32 devices in a mesh: groups: 2 (over y), dp: 16 (over z, x, core).
Axes of the slice: x: 2, y: 2, z: 4, core: 2. Of those that a mesh axis runs over, the one named last changes fastest.
Arguments:
- particles: bfloat16 [2048, 128, 128], P(('groups', 'dp')), parts along dimension 0, may hold values from -20 to 20
- refs: bfloat16 [128, 256, 128], P('dp', 'groups'), parts along dimension 1, may hold values from -0.5 to 0.5
- ctf_group: int32 [2048], P(('groups', 'dp')), parts along dimension 0, may hold values from 0 to 31, as said below
- defocus: float32 [64], P('groups'), parts along dimension 0, may hold values from 0.5 to 2
- class_prior: float32 [256], P('groups'), parts along dimension 0, may hold values from 0.25 to 4
- cycle_weight: float32 [64], replicated, may hold values from 0.5 to 2
Outputs:
- new_refs: float32 [128, 256, 128], P('dp', 'groups'), parts along dimension 1
- log_evidence: float32 [2048], P(('groups', 'dp')), parts along dimension 0
The draws below stay inside these ranges and needn't reach their ends.
There are 2 independent parts, one for each index of `groups`. The reference program is written for one: setup_inputs(seed, part) draws one part's arguments, and reference() takes and returns one part's arrays. A program takes and returns all parts, laid end to end along the dimension named above; an argument that names none is the same for every part. Nothing has to cross between parts.
Inputs may be any that keep to these rules, and one draw needn't show every extreme that they name: `ctf_group`: CTF groups follow the particle order: particle n belongs to group n * 32 // 1024 or the next one, capped at 31.
All inputs are finite; a program needn't handle non-finite values.
Results may differ from the reference program's by a relative error of at most 0.0045.
Values may be sent and summed in bfloat16 or wider, within the bound.
No kernel may reach another device: no remote copies, remote signals or barrier semaphores. Data moves between devices by JAX's collectives and lax.ppermute only.
A program may use at most 64 MiB of HBM per device.

```python
import math
import jax
import jax.numpy as jnp
from jax import lax

M = 128
R = 64
K = 128
ROT = 36
G = 32
NP_DEV = 64
NALL = 1024


def ctf_values(defocus):
    radius = (jnp.arange(R, dtype=jnp.float32) + 1.0) / R
    phase = 20.0 * defocus[:, None] * radius[None, :] ** 2
    return -(0.995 * jnp.sin(phase) + 0.1 * jnp.cos(phase))


def shared_draw(key):
    key_ref = jax.random.fold_in(key, 11)
    key_label = jax.random.fold_in(key, 12)
    key_group = jax.random.fold_in(key, 13)
    key_focus = jax.random.fold_in(key, 14)
    key_noise = jax.random.fold_in(key, 15)
    index = jnp.arange(NALL, dtype=jnp.int32)
    base = index * G // NALL + jax.random.randint(key_group, (NALL,), 0, 2)
    ctf_group = jnp.minimum(base, G - 1).astype(jnp.int32)
    labels = jax.random.randint(key_label, (NALL,), 0, K)
    refs = jnp.clip(jax.random.normal(key_ref, (M, K, 2 * R), jnp.float32), -6.0, 6.0) / 64.0
    amplitude = jnp.full((NALL,), 4.0, jnp.float32)
    defocus = jnp.exp(jax.random.uniform(key_focus, (G,), jnp.float32, math.log(0.5), math.log(2.0)))
    noise = jnp.clip(jax.random.normal(key_noise, (NALL, M, 2 * R), jnp.float32), -6.0, 6.0)
    ctf = ctf_values(defocus)
    gain = jnp.concatenate([ctf, ctf], axis=1)[ctf_group]
    signal = jnp.take(jnp.transpose(refs, (1, 0, 2)), labels, axis=0)
    particles = amplitude[:, None, None] * gain[:, None, :] * signal + noise
    return (particles, refs, ctf_group, defocus)


def draw_particles(key, part):
    return shared_draw(key)[0].astype(jnp.bfloat16)


def draw_refs(key, part):
    return shared_draw(key)[1].astype(jnp.bfloat16)


def draw_ctf_group(key, part):
    return shared_draw(key)[2]


def draw_defocus(key, part):
    return shared_draw(key)[3]


def setup_inputs(seed: int = 0, part: int = 0) -> dict:
    keys = jax.random.split(jax.random.key(seed), 7)
    part_keys = jax.random.split(jax.random.fold_in(keys[6], part), 7)
    return {
        "particles": draw_particles(jax.random.fold_in(jax.random.fold_in(keys[6], part), 71), part),
        "refs": draw_refs(jax.random.fold_in(jax.random.fold_in(keys[6], part), 71), part),
        "ctf_group": draw_ctf_group(jax.random.fold_in(jax.random.fold_in(keys[6], part), 71), part),
        "defocus": draw_defocus(jax.random.fold_in(jax.random.fold_in(keys[6], part), 71), part),
        "class_prior": jnp.clip(jnp.exp(jax.random.uniform(part_keys[4], (K,), jnp.float32, math.log(0.25), math.log(4.0))), 0.25, 4.0),
        "cycle_weight": jnp.clip(jnp.exp(jax.random.uniform(keys[5], (R,), jnp.float32, math.log(0.5), math.log(2.0))), 0.5, 2.0),
    }


def ctf_table(defocus):
    radius = (jnp.arange(R, dtype=jnp.float32) + 1.0) / R
    phase = 20.0 * defocus[:, None] * radius[None, :] ** 2
    return -(0.995 * jnp.sin(phase) + 0.1 * jnp.cos(phase))


def angle_tables():
    harmonic = jnp.arange(M, dtype=jnp.float32)[:, None]
    turning = jnp.arange(ROT, dtype=jnp.float32)[None, :]
    theta = 2.0 * math.pi * harmonic * turning / ROT
    return jnp.cos(theta), jnp.sin(theta)


def reference(particles, refs, ctf_group, defocus, class_prior, cycle_weight):
    highest = lax.Precision.HIGHEST
    ctf = ctf_table(defocus)
    cos_table, sin_table = angle_tables()
    refs_wide = refs.astype(jnp.float32)
    energy = jnp.sum(refs_wide[:, :, :R] ** 2 + refs_wide[:, :, R:] ** 2, axis=0)
    quadratic = jnp.dot(cycle_weight[None, :] * ctf * ctf, energy.T, precision=highest)
    log_prior = jnp.log(class_prior)
    gain_table = jnp.concatenate([cycle_weight[None, :] * ctf, cycle_weight[None, :] * ctf], axis=1)

    def block_step(totals, inputs):
        numer, mass = totals
        images, labels = inputs
        onehot = (labels[:, None] == jnp.arange(G, dtype=jnp.int32)[None, :]).astype(jnp.float32)
        gain = jnp.dot(onehot, gain_table, precision=highest)
        weighted = (images.astype(jnp.float32) * gain[:, None, :]).astype(jnp.bfloat16)
        turned = jnp.concatenate([weighted[:, :, R:], -weighted[:, :, :R]], axis=2)
        wide_weighted = weighted.astype(jnp.float32)
        wide_turned = turned.astype(jnp.float32)
        cross_real = jnp.einsum('nmq,mkq->mnk', wide_weighted, refs_wide, precision=highest)
        cross_imag = jnp.einsum('nmq,mkq->mnk', wide_turned, refs_wide, precision=highest)
        corr = jnp.einsum('mnk,mj->nkj', cross_real, cos_table, precision=highest)
        corr = corr - jnp.einsum('mnk,mj->nkj', cross_imag, sin_table, precision=highest)
        norm_term = jnp.dot(onehot, quadratic, precision=highest)
        scores = corr - 0.5 * norm_term[:, :, None] + log_prior[None, :, None]
        flat = scores.reshape(scores.shape[0], K * ROT)
        top = jnp.max(flat, axis=1, keepdims=True)
        expo = jnp.exp(flat - top)
        total = jnp.sum(expo, axis=1, keepdims=True)
        posterior = (expo / total).reshape(scores.shape)
        evidence = top[:, 0] + jnp.log(total[:, 0])
        mass = mass + jnp.dot(onehot.T, jnp.sum(posterior, axis=2), precision=highest)
        post_real = jnp.einsum('nkj,mj->mnk', posterior, cos_table, precision=highest).astype(jnp.bfloat16)
        post_imag = jnp.einsum('nkj,mj->mnk', posterior, sin_table, precision=highest).astype(jnp.bfloat16)
        numer = numer + jnp.einsum('mnk,nmq->mkq', post_real.astype(jnp.float32), wide_weighted, precision=highest)
        numer = numer - jnp.einsum('mnk,nmq->mkq', post_imag.astype(jnp.float32), wide_turned, precision=highest)
        return (numer, mass), evidence

    blocks = NALL // NP_DEV
    images_all = particles.reshape(blocks, NP_DEV, M, 2 * R)
    labels_all = ctf_group.reshape(blocks, NP_DEV)
    start_numer = jnp.zeros((M, K, 2 * R), jnp.float32)
    start_mass = jnp.zeros((G, K), jnp.float32)
    (numer, mass), evidence = lax.scan(block_step, (start_numer, start_mass), (images_all, labels_all))
    denom = 1.0 + jnp.dot(mass.T, cycle_weight[None, :] * ctf * ctf, precision=highest)
    denom_wide = jnp.concatenate([denom, denom], axis=1)
    new_refs = numer / denom_wide[None, :, :]
    return new_refs, evidence.reshape(NALL)
```

```python
import functools
import math

import jax
import jax.numpy as jnp
import numpy as np
from jax import lax
from jax.experimental import pallas as pl
from jax.experimental.pallas import tpu as pltpu
from jax.sharding import PartitionSpec as P

ROT = 36
HALF = ROT // 2
HIGHEST = lax.Precision.HIGHEST
F32 = jnp.float32
BF16 = jnp.bfloat16
VMEM_LIMIT = 40 * 1024 * 1024


def chip_ring(mesh):
    chips = mesh.shape["dp"] // 2
    wide = 2
    coords = [getattr(d, "coords", None) for d in mesh.devices.reshape(-1, chips * 2)[0]]
    if all(c is not None for c in coords):
        wide = len({c[0] for c in coords})
    if chips % wide:
        wide = 1
    deep = chips // wide
    if wide == 1:
        return list(range(chips))
    ring = []
    for z in range(deep):
        xs = range(1, wide) if z % 2 == 0 else range(wide - 1, 0, -1)
        ring += [z * wide + x for x in xs]
    ring += [z * wide for z in range(deep - 1, -1, -1)]
    return ring


def ring_perm(ring, shift, cross):
    n = len(ring)
    pairs = []
    for at, chip in enumerate(ring):
        to = ring[(at + shift) % n]
        pairs += [(2 * chip + c, 2 * to + (c ^ cross)) for c in (0, 1)]
    return pairs


def _combine(terms):
    by = {}
    for k, v in terms:
        k %= ROT
        k = min(k, ROT - k)
        sign = 1
        if k > 9:
            k, sign = HALF - k, -1
        if k == 9:
            continue
        by.setdefault(k, []).append((sign, v))
    total = None
    for k, vs in sorted(by.items()):
        part, psign = None, 1
        for sign, v in vs:
            if part is None:
                part, psign = v, sign
            else:
                part = part + v if sign == psign else part - v
        if k:
            part = part * math.cos(k * math.pi / HALF)
        if total is None:
            total = part if psign > 0 else -part
        else:
            total = total + part if psign > 0 else total - part
    return total


def cos_transform(a):
    plus = [a[t] + a[HALF - t] for t in range(9)] + [a[9]]
    minus = [a[t] - a[HALF - t] for t in range(9)]
    out = [None] * 19
    for j in range(10):
        side = plus if j % 2 == 0 else minus
        even = _combine([(t * j, side[t]) for t in range(0, len(side), 2)])
        odd = _combine([(t * j, side[t]) for t in range(1, len(side), 2)])
        if odd is None:
            out[j] = out[HALF - j] = even
        else:
            out[j] = even + odd
            out[HALF - j] = even - odd
    return out


def sin_transform(b):
    plus = {t: b[t] + b[HALF - t] for t in range(1, 9)}
    plus[9] = b[9]
    minus = {t: b[t] - b[HALF - t] for t in range(1, 9)}
    out = [None] * 18
    for j in range(1, 10):
        side = plus if j % 2 else minus
        even = _combine([(9 - t * j, v) for t, v in side.items() if t % 2 == 0])
        odd = _combine([(9 - t * j, v) for t, v in side.items() if t % 2])
        if odd is None:
            odd = jnp.zeros_like(even)
        if even is None:
            even = jnp.zeros_like(odd)
        out[j] = odd + even
        if j != 9:
            out[HALF - j] = odd - even
    return out


def _residue(m):
    r = lax.rem(m, ROT)
    flip = r > HALF
    return jnp.where(flip, ROT - r, r), jnp.where(flip, -1.0, 1.0).astype(F32)


def _half_sign(shape):
    lane = lax.broadcasted_iota(jnp.int32, shape, len(shape) - 1)
    return jnp.where(lane < shape[-1] // 2, -1.0, 1.0).astype(F32)


def _forward(base, piece, wo, ws, acc, energy):
    mp, kh, q = piece.shape
    sign = _half_sign((kh, q))
    squares = jnp.zeros((kh, q), F32)
    for j in range(mp):
        t, s = _residue(base * mp + j)
        x = piece[j]
        wide = x.astype(F32)
        squares = squares + wide * wide
        swapped = (pltpu.roll(wide, q // 2, 1) * sign).astype(BF16)
        both = jnp.concatenate([x, swapped], axis=0)
        w = jnp.concatenate([wo[j], ws[j]], axis=0)
        y = lax.dot_general(both, w, (((1,), (1,)), ((), ())), preferred_element_type=F32)
        acc[t, :kh, :] += y[:kh]
        acc[t, kh:, :] += s * y[kh:]
    energy[...] += squares


def _backward(base, table, wo, ws, j, mp):
    t, s = _residue(base * mp + j)
    w = jnp.concatenate([wo[j], ws[j]], axis=0)
    y = jnp.dot(table[t], w, preferred_element_type=F32)
    kh = y.shape[0] // 2
    turned = pltpu.roll(y[kh:], y.shape[1] // 2, 1) * (_half_sign((kh, y.shape[1])) * s)
    return y[:kh] + turned


def forward_kernel(count, first, ids, *refs):
    pieces, rest = refs[:count], refs[count:]
    wos, wss, rest = rest[:count], rest[count : 2 * count], rest[2 * count :]
    if first:
        acc, energy = rest
        acc[...] = jnp.zeros_like(acc)
        energy[...] = jnp.zeros_like(energy)
    else:
        acc_in, energy_in, acc, energy = rest
        acc[...] = acc_in[...]
        energy[...] = energy_in[...]
    for i in range(count):
        _forward(ids[i], pieces[i], wos[i], wss[i], acc, energy)


def score_kernel(count, ids, *refs):
    pieces, rest = refs[:count], refs[count:]
    wos, wss, rest = rest[:count], rest[count : 2 * count], rest[2 * count :]
    acc_in, energy_in, w2, prior, real_out, imag_out, stats, acc, energy, scores = rest
    acc[...] = acc_in[...]
    energy[...] = energy_in[...]
    for i in range(count):
        _forward(ids[i], pieces[i], wos[i], wss[i], acc, energy)
    kh, n = scores.shape[1:]
    norm = lax.dot_general(
        energy[...], w2[...], (((1,), (1,)), ((), ())), precision=HIGHEST, preferred_element_type=F32
    )
    energy[...] = jnp.log(prior[...]) - 0.5 * norm
    tile = 8

    def scan_scores(i, top):
        at = pl.multiple_of(i * tile, tile)
        rows, rows_imag = pl.ds(at, tile), pl.ds(pl.multiple_of(kh + i * tile, tile), tile)
        p = cos_transform([acc[t, rows, :] for t in range(19)])
        q = sin_transform([None] + [acc[t, rows_imag, :] for t in range(1, HALF)])
        base = energy[rows, :]
        for j in range(19):
            pj = p[j] + base
            if j in (0, HALF):
                scores[j, rows, :] = pj
                top = jnp.maximum(top, pj)
            else:
                lo, hi = pj - q[j], pj + q[j]
                scores[j, rows, :] = lo
                scores[ROT - j, rows, :] = hi
                top = jnp.maximum(top, jnp.maximum(lo, hi))
        return top

    top = lax.fori_loop(0, kh // tile, scan_scores, jnp.full((tile, n), -jnp.inf, F32))
    top = jnp.max(top, axis=0, keepdims=True)

    def scan_exp(i, total):
        rows = pl.ds(pl.multiple_of(i * tile, tile), tile)
        u = [jnp.exp(scores[j, rows, :] - top) for j in range(ROT)]
        plus = [u[0]] + [u[j] + u[ROT - j] for j in range(1, HALF)] + [u[HALF]]
        minus = [None] + [u[j] - u[ROT - j] for j in range(1, HALF)]
        real = cos_transform(plus)
        imag = sin_transform(minus)
        for t in range(19):
            real_out[t, rows, :] = real[t]
        for t in range(1, HALF):
            imag_out[t - 1, rows, :] = imag[t]
        return total + real[0]

    total = lax.fori_loop(0, kh // tile, scan_exp, jnp.zeros((tile, n), F32))
    stats[0:1, :] = top
    stats[1:2, :] = jnp.sum(total, axis=0, keepdims=True)


def table_kernel(count, ids, real, imag, mine, other, w2, *refs):
    wos, wss, rest = refs[:count], refs[count : 2 * count], refs[2 * count :]
    table, evidence, dpart, outs = rest[0], rest[1], rest[2], rest[3:]
    kh, n = real.shape[1:]
    theirs = pltpu.roll(jnp.broadcast_to(other[...].reshape(2, 1, n), (2, 8, n)).reshape(16, n), n // 2, 1)
    top_a, total_a = mine[0:1, :], mine[1:2, :]
    top_b, total_b = theirs[0:1, :], theirs[8:9, :]
    top = jnp.maximum(top_a, top_b)
    scale = jnp.exp(top_a - top)
    total = total_a * scale + total_b * jnp.exp(top_b - top)
    evidence[...] = top + jnp.log(total)
    scale = scale / total
    for t in range(19):
        table[t, :kh, :] = (real[t] * scale).astype(BF16)
        if 0 < t < HALF:
            table[t, kh:, :] = (imag[t - 1] * scale).astype(BF16)
        else:
            table[t, kh:, :] = jnp.zeros((kh, n), BF16)
    dpart[...] = jnp.dot(real[0] * scale, w2[...], precision=HIGHEST, preferred_element_type=F32)
    for i in range(count):
        mp = outs[i].shape[0]
        for j in range(mp):
            outs[i][j] = _backward(ids[i], table, wos[i], wss[i], j, mp).astype(outs[i].dtype)


def numer_kernel(count, init, ids, table, *refs):
    wos, wss, rest = refs[:count], refs[count : 2 * count], refs[2 * count :]
    inits, outs = (rest[:count], rest[count:]) if init else (None, rest)
    for i in range(count):
        mp = outs[i].shape[0]
        for j in range(mp):
            y = _backward(ids[i], table, wos[i], wss[i], j, mp)
            if init:
                y = y + inits[i][j].astype(F32)
            outs[i][j] = y.astype(outs[i].dtype)


def final_kernel(ids, own, left, right, own_x, left_x, right_x, dsum, dsum_x, out):
    kh = own.shape[1]
    c = ids[0]
    near = pl.ds(pl.multiple_of(c * kh, kh), kh)
    far = pl.ds(pl.multiple_of((1 - c) * kh, kh), kh)
    inv, inv_x = 1.0 / (1.0 + dsum[...]), 1.0 / (1.0 + dsum_x[...])
    for j in range(own.shape[0]):
        out[j, near, :] = (own[j] + left[j].astype(F32) + right[j].astype(F32)) * inv
        out[j, far, :] = (own_x[j].astype(F32) + left_x[j].astype(F32) + right_x[j].astype(F32)) * inv_x


def _call(kernel, ids, operands, w_at, w, outs, scratch=(), cost=1_000_000, aliases=None):
    wo, ws = w
    mp = None
    specs = []
    full = lambda a: pl.BlockSpec(a.shape, lambda g, s, nd=a.ndim: (0,) * nd)
    args = []
    for a in operands[:w_at[0]]:
        specs.append(full(a))
        args.append(a)
    count = w_at[1]
    if count:
        mp = w_at[2]
        for arr in (wo, ws):
            for i in range(count):
                specs.append(pl.BlockSpec((mp,) + arr.shape[1:], lambda g, s, i=i: (s[i], 0, 0)))
                args.append(arr)
    for a in operands[w_at[0] :]:
        specs.append(full(a))
        args.append(a)
    nbytes = sum(math.prod(o.shape) * o.dtype.itemsize for o in outs)
    return pl.pallas_call(
        kernel,
        out_shape=outs,
        grid_spec=pltpu.PrefetchScalarGridSpec(
            num_scalar_prefetch=1,
            grid=(1,),
            in_specs=specs,
            out_specs=[pl.BlockSpec(o.shape, lambda g, s, nd=len(o.shape): (0,) * nd) for o in outs],
            scratch_shapes=scratch,
        ),
        compiler_params=pltpu.CompilerParams(vmem_limit_bytes=VMEM_LIMIT),
        cost_estimate=pl.CostEstimate(flops=cost, bytes_accessed=2 * nbytes, transcendentals=0),
    )(ids, *args)


def ctf_table(defocus, radial):
    radius = (jnp.arange(radial, dtype=F32) + 1.0) / radial
    phase = 20.0 * defocus[:, None] * radius[None, :] ** 2
    return -(0.995 * jnp.sin(phase) + 0.1 * jnp.cos(phase))


def shards(ring, particles, refs, ctf_group, defocus, class_prior, cycle_weight):
    chips = len(ring)
    opposite = chips // 2
    nl, _, q = particles.shape
    mp, k, _ = refs.shape
    kh = k // 2
    n2 = 2 * nl
    me = lax.axis_index("dp")
    c = lax.rem(me, 2)
    chip_at = np.zeros((2 * chips, chips), np.int32)
    for at, chip in enumerate(ring):
        for core in (0, 1):
            chip_at[2 * chip + core] = [ring[(at + s) % chips] for s in range(chips)]
    at_distance = lax.dynamic_index_in_dim(jnp.asarray(chip_at), me, 0, keepdims=False)

    def dev(s, cross):
        return 2 * at_distance[s % chips] + (c ^ cross)

    def ids_of(pairs):
        return jnp.stack([dev(s, x) for s, x in pairs]).astype(jnp.int32)

    swap = [(i, i ^ 1) for i in range(2 * chips)]
    send = lambda a, shift, cross: lax.ppermute(a, "dp", ring_perm(ring, shift, cross))
    core_swap = lambda a: lax.ppermute(a, "dp", swap)

    near = lax.dynamic_slice_in_dim(refs, c * kh, kh, axis=1)
    far = lax.dynamic_slice_in_dim(refs, (1 - c) * kh, kh, axis=1)
    from_left = [send(near, 1, 0), send(far, 1, 1)]
    from_right = [send(near, -1, 0), send(far, -1, 1)]
    sister = core_swap(far)

    group_x = core_swap(ctf_group)
    ctf = ctf_table(defocus, q // 2)
    gains = cycle_weight[None, :] * ctf
    gain_table = jnp.concatenate([gains, gains], axis=1)
    square_table = jnp.concatenate([gains * ctf, gains * ctf], axis=1)
    groups = jnp.concatenate([ctf_group, group_x])
    index = jnp.arange(defocus.shape[0], dtype=jnp.int32)[None, :]
    onehot = (ctf_group[:, None] == index).astype(F32)
    gain = jnp.dot(onehot, gain_table, precision=HIGHEST)
    onehot_all = (groups[:, None] == index).astype(F32)
    w2 = jnp.dot(onehot_all, square_table, precision=HIGHEST)
    wo = jnp.transpose((particles.astype(F32) * gain[:, None, :]).astype(BF16), (1, 0, 2))
    ws = core_swap(wo)
    w = (wo, ws)
    prior = lax.dynamic_slice_in_dim(class_prior, c * kh, kh, axis=0)[:, None]
    prior = jnp.broadcast_to(prior, (kh, n2))

    shape = jax.ShapeDtypeStruct
    acc_shapes = [shape((19, 2 * kh, n2), F32), shape((kh, q), F32)]
    pieces, where = [near, sister], [(0, 0), (0, 1)]
    acc = None
    for step in range(1, opposite + 1):
        pieces += from_left + from_right
        if step < opposite:
            where += [(-step, 0), (-step, 1), (step, 0), (step, 1)]
        else:
            where += [(step, 0), (step, 1)]
        if step < opposite - 1:
            from_left_next = [send(a, 1, 0) for a in from_left]
            from_right_next = [send(a, -1, 0) for a in from_right]
        elif step == opposite - 1:
            from_left_next = [send(from_left[0], 1, 0)]
            from_right_next = [send(from_right[1], -1, 0)]
        if step == opposite:
            break
        from_left, from_right = from_left_next, from_right_next
        count = len(pieces)
        body = functools.partial(forward_kernel, count, acc is None)
        acc = _call(
            body,
            ids_of(where),
            pieces + ([] if acc is None else list(acc)),
            (count, count, mp),
            w,
            acc_shapes,
            cost=count * mp * 2 * q * n2 * 2 * kh * 4,
        )
        pieces, where = [], []

    count = len(pieces)
    table_f32 = [shape((19, kh, n2), F32), shape((17, kh, n2), F32), shape((2, n2), F32)]
    real, imag, stats = _call(
        functools.partial(score_kernel, count),
        ids_of(where),
        pieces + list(acc) + [w2, prior],
        (count, count, mp),
        w,
        table_f32,
        scratch=[
            pltpu.VMEM((19, 2 * kh, n2), F32),
            pltpu.VMEM((kh, q), F32),
            pltpu.VMEM((ROT, kh, n2), F32),
        ],
        cost=100_000_000,
    )
    stats_x = core_swap(stats)

    piece = shape((mp, kh, q), BF16)
    wide_piece = shape((mp, kh, q), F32)
    table, evidence, dsum, to_right, to_left = _call(
        functools.partial(table_kernel, 2),
        ids_of([(opposite, 0), (opposite, 1)]),
        [real, imag, stats, stats_x, w2],
        (5, 2, mp),
        w,
        [shape((19, 2 * kh, n2), BF16), shape((1, n2), F32), shape((kh, q), F32), piece, piece],
        cost=50_000_000,
    )
    sent_right, sent_left = [to_right], [to_left]
    here = None
    for step in range(1, opposite + 1):
        if step < opposite or opposite == 1:
            pass
        if step == 1:
            got_left = [send(sent_right[0], 1, 0)]
            got_right = [send(sent_left[0], -1, 0)]
        elif step < opposite:
            got_left = [send(a, 1, 0) for a in sent_right]
            got_right = [send(a, -1, 0) for a in sent_left]
        dist = opposite - step
        if dist == 0:
            break
        new_right, new_left = [None, None], [None, None]
        for x in (0, 1):
            spots, inits = [(dist, x), (-dist, x)], [None, None]
            if step == 1:
                if x == 0:
                    inits[0] = got_left[0]
                else:
                    inits[1] = got_right[0]
            else:
                inits = [got_left[x], got_right[x]]
            with_init = [i for i in (0, 1) if inits[i] is not None]
            if len(with_init) == 2:
                res = _call(
                    functools.partial(numer_kernel, 2, True),
                    ids_of(spots),
                    [table] + inits,
                    (1, 2, mp),
                    w,
                    [piece, piece],
                )
            else:
                res = [None, None]
                for i in (0, 1):
                    ini = inits[i] is not None
                    res[i] = _call(
                        functools.partial(numer_kernel, 1, ini),
                        ids_of([spots[i]]),
                        [table] + ([inits[i]] if ini else []),
                        (1, 1, mp),
                        w,
                        [piece],
                    )[0]
            new_right[x], new_left[x] = res
        sent_right, sent_left = new_right, new_left
    own, own_far = _call(
        functools.partial(numer_kernel, 2, False),
        ids_of([(0, 0), (0, 1)]),
        [table],
        (1, 2, mp),
        w,
        [wide_piece, piece],
    )
    own_x = core_swap(own_far)
    left, left_x = send(sent_right[0], 1, 0), send(sent_right[1], 1, 1)
    right, right_x = send(sent_left[0], -1, 0), send(sent_left[1], -1, 1)

    if chips & (chips - 1) == 0:
        bit = 2
        while bit < 2 * chips:
            dsum = dsum + lax.ppermute(dsum, "dp", [(i, i ^ bit) for i in range(2 * chips)])
            bit *= 2
    else:
        halves = [[2 * i + core for i in range(chips)] for core in (0, 1)]
        dsum = lax.psum(dsum, "dp", axis_index_groups=halves)
    dsum_x = core_swap(dsum)

    new_refs = _call(
        final_kernel,
        c[None].astype(jnp.int32),
        [own, left, right, own_x, left_x, right_x, dsum, dsum_x],
        (8, 0, mp),
        w,
        [shape((mp, k, q), F32)],
    )[0]
    return new_refs, evidence[0, :nl]


def solution(mesh):
    in_specs = (
        P(("groups", "dp"), None, None),
        P("dp", "groups", None),
        P(("groups", "dp")),
        P("groups"),
        P("groups"),
        P(),
    )
    out_specs = (P("dp", "groups", None), P(("groups", "dp")))
    body = functools.partial(shards, chip_ring(mesh))
    return jax.shard_map(body, mesh=mesh, in_specs=in_specs, out_specs=out_specs, check_vma=False)
```

```python
import functools
import math

import jax
import jax.numpy as jnp
from jax import lax
from jax.experimental import pallas as pl
from jax.experimental.layout import Layout, with_layout_constraint
from jax.experimental.pallas import tpu as pltpu
from jax.sharding import PartitionSpec as P

ROT = 36
HALF = ROT // 2
HIGHEST = lax.Precision.HIGHEST
F32 = jnp.float32
BF16 = jnp.bfloat16
VMEM_LIMIT = 40 * 1024 * 1024


class Ring:
    def __init__(self, mesh):
        self.chips = mesh.shape["dp"] // 2
        wide = 2
        coords = [getattr(d, "coords", None) for d in mesh.devices.reshape(-1, 2 * self.chips)[0]]
        if all(c is not None for c in coords):
            wide = len({c[0] for c in coords})
        self.wide = wide if self.chips % wide == 0 else 1
        self.deep = self.chips // self.wide

    def chip(self, pos, div=lambda a, b: a // b, pick=lambda c, a, b: a if c else b):
        if self.wide == 1:
            return pos
        row = self.wide - 1
        z = div(pos, row)
        i = pos - z * row
        x = pick(z - 2 * div(z, 2) == 0, 1 + i, row - i)
        back = self.deep - 1 - (pos - self.deep * row)
        return pick(pos < self.deep * row, z * self.wide + x, back * self.wide)

    def pos(self, chip, div=lambda a, b: a // b, pick=lambda c, a, b: a if c else b):
        if self.wide == 1:
            return chip
        row = self.wide - 1
        z = div(chip, self.wide)
        x = chip - z * self.wide
        i = pick(z - 2 * div(z, 2) == 0, x - 1, row - x)
        return pick(x == 0, self.deep * row + self.deep - 1 - z, z * row + i)

    def order(self):
        return [self.chip(p) for p in range(self.chips)]

    def devices(self, spots):
        me = lax.axis_index("dp")
        at = self.pos(lax.div(me, 2), lax.div, jnp.where)
        core = me - 2 * lax.div(me, 2)
        found = []
        for dist, other in spots:
            chip = self.chip(lax.rem(at + dist % self.chips, self.chips), lax.div, jnp.where)
            found.append(2 * chip + (1 - core if other else core))
        return found, core


def ring_perm(ring, shift, cross):
    n = len(ring)
    pairs = []
    for at, chip in enumerate(ring):
        to = ring[(at + shift) % n]
        pairs += [(2 * chip + c, 2 * to + (c ^ cross)) for c in (0, 1)]
    return pairs


def _combine(terms):
    by = {}
    for k, v in terms:
        k %= ROT
        k = min(k, ROT - k)
        sign = 1
        if k > 9:
            k, sign = HALF - k, -1
        if k == 9:
            continue
        by.setdefault(k, []).append((sign, v))
    total = None
    for k, vs in sorted(by.items()):
        part, psign = None, 1
        for sign, v in vs:
            if part is None:
                part, psign = v, sign
            else:
                part = part + v if sign == psign else part - v
        if k:
            part = part * math.cos(k * math.pi / HALF)
        if total is None:
            total = part if psign > 0 else -part
        else:
            total = total + part if psign > 0 else total - part
    return total


def cos_transform(a):
    plus = [a[t] + a[HALF - t] for t in range(9)] + [a[9]]
    minus = [a[t] - a[HALF - t] for t in range(9)]
    out = [None] * 19
    for j in range(10):
        side = plus if j % 2 == 0 else minus
        even = _combine([(t * j, side[t]) for t in range(0, len(side), 2)])
        odd = _combine([(t * j, side[t]) for t in range(1, len(side), 2)])
        if odd is None:
            out[j] = out[HALF - j] = even
        else:
            out[j] = even + odd
            out[HALF - j] = even - odd
    return out


def sin_transform(b):
    plus = {t: b[t] + b[HALF - t] for t in range(1, 9)}
    plus[9] = b[9]
    minus = {t: b[t] - b[HALF - t] for t in range(1, 9)}
    out = [None] * 18
    for j in range(1, 10):
        side = plus if j % 2 else minus
        even = _combine([(9 - t * j, v) for t, v in side.items() if t % 2 == 0])
        odd = _combine([(9 - t * j, v) for t, v in side.items() if t % 2])
        if odd is None:
            odd = jnp.zeros_like(even)
        if even is None:
            even = jnp.zeros_like(odd)
        out[j] = odd + even
        if j != 9:
            out[HALF - j] = odd - even
    return out


def _residue(m):
    r = lax.rem(m, ROT)
    flip = r > HALF
    return jnp.where(flip, ROT - r, r), jnp.where(flip, -1.0, 1.0).astype(F32)


def _half_sign(shape):
    lane = lax.broadcasted_iota(jnp.int32, shape, len(shape) - 1)
    return jnp.where(lane < shape[-1] // 2, -1.0, 1.0).astype(F32)


def _forward(base, mp, piece, row, wo, ws, acc, energy):
    kh, q = piece.shape[1:]
    sign = _half_sign((kh, q))
    first = base * mp
    squares = jnp.zeros((kh, q), F32)
    for j in range(mp):
        m = first + j
        t, s = _residue(m)
        x = piece[row + j]
        wide = x.astype(F32)
        squares = squares + wide * wide
        swapped = (pltpu.roll(wide, q // 2, 1) * sign).astype(BF16)
        both = jnp.concatenate([x, swapped], axis=0)
        w = jnp.concatenate([wo[m], ws[m]], axis=0)
        y = lax.dot_general(both, w, (((1,), (1,)), ((), ())), preferred_element_type=F32)
        acc[t, :kh, :] += y[:kh]
        acc[t, kh:, :] += s * y[kh:]
    energy[...] += squares


def _backward(m, table, wo, ws):
    t, s = _residue(m)
    w = jnp.concatenate([wo[m], ws[m]], axis=0)
    y = jnp.dot(table[t], w, preferred_element_type=F32)
    kh = y.shape[0] // 2
    turned = pltpu.roll(y[kh:], y.shape[1] // 2, 1) * (_half_sign((kh, y.shape[1])) * s)
    return y[:kh] + turned


def forward_kernel(ring, spots, mp, first, wo, ws, *refs):
    acc, energy = refs[-2:]
    if first:
        acc[...] = jnp.zeros_like(acc)
        energy[...] = jnp.zeros_like(energy)
    at, _ = ring.devices([place for _, _, place in spots])
    for base, (operand, row, _) in zip(at, spots):
        _forward(base, mp, refs[operand], row, wo, ws, acc, energy)


def score_kernel(ring, spots, mp, wo, ws, *refs):
    at, _ = ring.devices([place for _, _, place in spots])
    w2, prior, _, _, acc, energy, real_out, imag_out, stats, scores = refs[2:]
    for base, (operand, row, _) in zip(at, spots):
        _forward(base, mp, refs[operand], row, wo, ws, acc, energy)
    kh, n = scores.shape[1:]
    norm = lax.dot_general(
        energy[...], w2[...], (((1,), (1,)), ((), ())), precision=HIGHEST, preferred_element_type=F32
    )
    energy[...] = jnp.log(prior[...]) - 0.5 * norm
    tile = 8

    def scan_scores(i, top):
        at = pl.multiple_of(i * tile, tile)
        rows, rows_imag = pl.ds(at, tile), pl.ds(pl.multiple_of(kh + i * tile, tile), tile)
        p = cos_transform([acc[t, rows, :] for t in range(19)])
        q = sin_transform([None] + [acc[t, rows_imag, :] for t in range(1, HALF)])
        base = energy[rows, :]
        for j in range(19):
            pj = p[j] + base
            if j in (0, HALF):
                scores[j, rows, :] = pj
                top = jnp.maximum(top, pj)
            else:
                lo, hi = pj - q[j], pj + q[j]
                scores[j, rows, :] = lo
                scores[ROT - j, rows, :] = hi
                top = jnp.maximum(top, jnp.maximum(lo, hi))
        return top

    top = lax.fori_loop(0, kh // tile, scan_scores, jnp.full((tile, n), -jnp.inf, F32))
    top = jnp.max(top, axis=0, keepdims=True)

    def scan_exp(i, total):
        rows = pl.ds(pl.multiple_of(i * tile, tile), tile)
        u = [jnp.exp(scores[j, rows, :] - top) for j in range(ROT)]
        plus = [u[0]] + [u[j] + u[ROT - j] for j in range(1, HALF)] + [u[HALF]]
        minus = [None] + [u[j] - u[ROT - j] for j in range(1, HALF)]
        real = cos_transform(plus)
        imag = sin_transform(minus)
        for t in range(19):
            real_out[t, rows, :] = real[t]
        for t in range(1, HALF):
            imag_out[t - 1, rows, :] = imag[t]
        return total + real[0]

    total = lax.fori_loop(0, kh // tile, scan_exp, jnp.zeros((tile, n), F32))
    stats[0:1, :] = top
    stats[1:2, :] = jnp.sum(total, axis=0, keepdims=True)


def table_kernel(ring, spots, mp, wo, ws, real, imag, mine, other, w2, table, evidence, dpart, *outs):
    kh, n = real.shape[1:]
    theirs = pltpu.roll(jnp.broadcast_to(other[...].reshape(2, 1, n), (2, 8, n)).reshape(16, n), n // 2, 1)
    top_a, total_a = mine[0:1, :], mine[1:2, :]
    top_b, total_b = theirs[0:1, :], theirs[8:9, :]
    top = jnp.maximum(top_a, top_b)
    scale = jnp.exp(top_a - top)
    total = total_a * scale + total_b * jnp.exp(top_b - top)
    evidence[...] = top + jnp.log(total)
    scale = scale / total
    for t in range(19):
        table[t, :kh, :] = (real[t] * scale).astype(BF16)
        if 0 < t < HALF:
            table[t, kh:, :] = (imag[t - 1] * scale).astype(BF16)
        else:
            table[t, kh:, :] = jnp.zeros((kh, n), BF16)
    dpart[...] = jnp.dot(real[0] * scale, w2[...], precision=HIGHEST, preferred_element_type=F32)
    at, _ = ring.devices(spots)
    for base, out in zip(at, outs):
        for j in range(mp):
            out[j] = _backward(base * mp + j, table, wo, ws).astype(out.dtype)
        out[mp] = _split(dpart[...])


def numer_kernel(ring, spots, mp, wo, ws, table, *outs):
    at, _ = ring.devices(spots)
    for i, base in enumerate(at):
        for j in range(mp):
            outs[i // 2][i % 2 * mp + j] = _backward(base * mp + j, table, wo, ws)


def _split(x):
    lead = x.astype(BF16)
    rest = (x - lead.astype(F32)).astype(BF16)
    lane = lax.broadcasted_iota(jnp.int32, x.shape, 1)
    return jnp.where(lane < x.shape[1] // 2, lead.astype(F32), rest.astype(F32)).astype(BF16)


def _join(row):
    wide = row.astype(F32)
    return wide + pltpu.roll(wide, row.shape[1] // 2, 1)


def add_kernel(mp, half, part_r, part_l, got_r, got_l, dsum, out_r, out_l, total):
    for side, (part, got, out) in enumerate(((part_r, got_r, out_r), (part_l, got_l, out_l))):
        for i in (0, 1):
            rows = slice(i * mp, (i + 1) * mp)
            y = part[rows]
            if not half:
                y = y + got[rows].astype(F32)
            elif i == side:
                y = y + got[:mp].astype(F32)
            out[rows] = y.astype(BF16)
        out[2 * mp] = got[got.shape[0] - 1]
    total[...] = dsum[...] + (_join(got_r[got_r.shape[0] - 1]) + _join(got_l[got_l.shape[0] - 1]))


def own_kernel(part, got_r, got_l, dsum, own, far):
    mp = own.shape[0]
    denom = 1.0 + dsum[...] + _join(got_r[2 * mp])
    inv = 1.0 / denom
    for j in range(2 * mp):
        y = (part[j] + got_r[j].astype(F32) + got_l[j].astype(F32)) * inv
        if j < mp:
            own[j] = y
        else:
            far[j - mp] = y.astype(BF16)


def final_kernel(ring, own, own_x, out):
    kh = own.shape[1]
    _, c = ring.devices([])
    out[:, pl.ds(pl.multiple_of(c * kh, kh), kh), :] = own[...]
    out[:, pl.ds(pl.multiple_of((1 - c) * kh, kh), kh), :] = own_x[...].astype(F32)


def _call(kernel, operands, outs, scratch=(), aliases=None, keep=True):
    return pl.pallas_call(
        kernel,
        out_shape=[pltpu.VMEM(o.shape, o.dtype) for o in outs] if keep else outs,
        in_specs=[pl.BlockSpec(memory_space=pltpu.VMEM)] * len(operands),
        out_specs=[pl.BlockSpec(memory_space=pltpu.VMEM)] * len(outs),
        scratch_shapes=scratch,
        input_output_aliases=aliases or {},
        compiler_params=pltpu.CompilerParams(vmem_limit_bytes=VMEM_LIMIT),
        cost_estimate=pl.CostEstimate(flops=1, bytes_accessed=1, transcendentals=0),
    )(*[pltpu.with_memory_space_constraint(a, pltpu.VMEM) for a in operands])


def ctf_table(defocus, radial):
    radius = (jnp.arange(radial, dtype=F32) + 1.0) / radial
    phase = 20.0 * defocus[:, None] * radius[None, :] ** 2
    return -(0.995 * jnp.sin(phase) + 0.1 * jnp.cos(phase))


def shards(ring, particles, refs, ctf_group, defocus, class_prior, cycle_weight):
    chips = ring.chips
    order = ring.order()
    opposite = chips // 2
    nl, _, q = particles.shape
    mp, k, _ = refs.shape
    kh = k // 2
    n2 = 2 * nl
    c = lax.rem(lax.axis_index("dp"), 2)

    send = lambda a, shift, cross: lax.ppermute(a, "dp", ring_perm(order, shift, cross))
    core_swap = lambda a: lax.ppermute(a, "dp", [(i, i ^ 1) for i in range(2 * chips)])
    tie = lax.optimization_barrier

    near = lax.dynamic_slice_in_dim(refs, c * kh, kh, axis=1)
    far = lax.dynamic_slice_in_dim(refs, (1 - c) * kh, kh, axis=1)
    group_x = core_swap(ctf_group)
    chunk = jnp.concatenate([near, core_swap(far)], axis=0)
    chunk, particles, defocus, cycle_weight, ctf_group = tie((chunk, particles, defocus, cycle_weight, ctf_group))
    from_left, from_right = send(chunk, 1, 0), send(chunk, -1, 0)
    particles_x = with_layout_constraint(core_swap(particles), Layout(major_to_minor=(0, 1, 2)))

    ctf = ctf_table(defocus, q // 2)
    gains = cycle_weight[None, :] * ctf
    gain_table = jnp.concatenate([gains, gains], axis=1)
    square_table = jnp.concatenate([gains * ctf, gains * ctf], axis=1)
    index = jnp.arange(defocus.shape[0], dtype=jnp.int32)[None, :]
    groups = jnp.concatenate([ctf_group, group_x])
    onehot = (groups[:, None] == index).astype(F32)
    both = jnp.dot(onehot, jnp.concatenate([gain_table, square_table], axis=1), precision=HIGHEST)
    gain, w2 = both[:, :q], both[:, q:]
    weigh = lambda a, g: jnp.transpose((a.astype(F32) * g[:, None, :]).astype(BF16), (1, 0, 2))
    wo = weigh(particles, gain[:nl])
    prior = lax.dynamic_slice_in_dim(class_prior, c * kh, kh, axis=0)[:, None]
    prior = jnp.broadcast_to(prior, (kh, n2))

    shape = jax.ShapeDtypeStruct
    acc_shapes = [shape((19, 2 * kh, n2), F32), shape((kh, q), F32)]
    pieces, where = [chunk], [(0, 0, (0, 0)), (0, mp, (0, 1))]
    acc = ws = None
    for step in range(1, opposite):
        for dist, got in ((-step, from_left), (step, from_right)):
            where += [(len(pieces), 0, (dist, 0)), (len(pieces), mp, (dist, 1))]
            pieces.append(got)
        if ws is None:
            from_left, from_right, wo, particles_x = tie((from_left, from_right, wo, particles_x))
            ws = weigh(particles_x, gain[nl:])
        elif acc is None:
            from_left, from_right, ws = tie((from_left, from_right, ws))
        else:
            from_left, from_right, acc = tie((from_left, from_right, acc))
        if step == opposite - 1:
            from_left, from_right = from_left[:mp], from_right[mp:]
        from_left, from_right = send(from_left, 1, 0), send(from_right, -1, 0)
        if step == 1 and opposite > 2:
            continue
        count = len(pieces)
        acc = _call(
            functools.partial(forward_kernel, ring, where, mp, acc is None),
            [wo, ws] + pieces + list(acc or []),
            acc_shapes,
            aliases={2 + count: 0, 3 + count: 1} if acc else None,
        )
        pieces, where = [], []

    where = [(0, 0, (opposite, 0)), (1, 0, (opposite, 1))]
    _, _, real, imag, stats = _call(
        functools.partial(score_kernel, ring, where, mp),
        [wo, ws, from_left, from_right, w2, prior] + list(acc),
        acc_shapes + [shape((19, kh, n2), F32), shape((17, kh, n2), F32), shape((2, n2), F32)],
        aliases={6: 0, 7: 1},
        scratch=[pltpu.VMEM((ROT, kh, n2), F32)],
    )
    stats_x = core_swap(stats)

    piece = shape((mp, kh, q), BF16)
    piece_d = shape((mp + 1, kh, q), BF16)
    pair = shape((2 * mp, kh, q), F32)
    pair_d = shape((2 * mp + 1, kh, q), BF16)
    dsum_shape = shape((kh, q), F32)
    table, evidence, dsum, to_right, to_left = _call(
        functools.partial(table_kernel, ring, [(opposite, 0), (opposite, 1)], mp),
        [wo, ws, real, imag, stats, stats_x, w2],
        [shape((19, 2 * kh, n2), BF16), shape((1, n2), F32), shape((kh, q), F32), piece_d, piece_d],
    )
    for dist in range(opposite - 1, -1, -1):
        got_r, got_l = send(to_right, 1, 0), send(to_left, -1, 0)
        spots = [(dist, 0), (dist, 1), (-dist, 0), (-dist, 1)] if dist else [(0, 0), (0, 1)]
        part = _call(functools.partial(numer_kernel, ring, spots, mp), [wo, ws, table], [pair] * (len(spots) // 2))
        if dist:
            to_right, to_left, dsum = _call(
                functools.partial(add_kernel, mp, dist == opposite - 1),
                [*part, got_r, got_l, dsum],
                [pair_d, pair_d, dsum_shape],
            )
    own, far = _call(own_kernel, [*part, got_r, got_l, dsum], [shape((mp, kh, q), F32), piece])
    new_refs = _call(
        functools.partial(final_kernel, ring), [own, core_swap(far)], [shape((mp, k, q), F32)], keep=False
    )[0]
    return new_refs, evidence[0, :nl]


def solution(mesh):
    in_specs = (
        P(("groups", "dp"), None, None),
        P("dp", "groups", None),
        P(("groups", "dp")),
        P("groups"),
        P("groups"),
        P(),
    )
    out_specs = (P("dp", "groups", None), P(("groups", "dp")))
    body = functools.partial(shards, Ring(mesh))
    return jax.shard_map(body, mesh=mesh, in_specs=in_specs, out_specs=out_specs, check_vma=False)
```

```python
import functools
import math

import jax
import jax.numpy as jnp
from jax import lax
from jax.experimental import pallas as pl
from jax.experimental.layout import Layout, with_layout_constraint
from jax.experimental.pallas import tpu as pltpu
from jax.sharding import PartitionSpec as P

ROT = 36
HALF = ROT // 2
HIGHEST = lax.Precision.HIGHEST
F32 = jnp.float32
BF16 = jnp.bfloat16
VMEM_LIMIT = 40 * 1024 * 1024


class Ring:
    def __init__(self, mesh):
        self.chips = mesh.shape["dp"] // 2
        wide = 2
        coords = [getattr(d, "coords", None) for d in mesh.devices.reshape(-1, 2 * self.chips)[0]]
        if all(c is not None for c in coords):
            wide = len({c[0] for c in coords})
        self.wide = wide if self.chips % wide == 0 else 1
        self.deep = self.chips // self.wide

    def chip(self, pos, div=lambda a, b: a // b, pick=lambda c, a, b: a if c else b):
        if self.wide == 1:
            return pos
        row = self.wide - 1
        z = div(pos, row)
        i = pos - z * row
        x = pick(z - 2 * div(z, 2) == 0, 1 + i, row - i)
        back = self.deep - 1 - (pos - self.deep * row)
        return pick(pos < self.deep * row, z * self.wide + x, back * self.wide)

    def pos(self, chip, div=lambda a, b: a // b, pick=lambda c, a, b: a if c else b):
        if self.wide == 1:
            return chip
        row = self.wide - 1
        z = div(chip, self.wide)
        x = chip - z * self.wide
        i = pick(z - 2 * div(z, 2) == 0, x - 1, row - x)
        return pick(x == 0, self.deep * row + self.deep - 1 - z, z * row + i)

    def order(self):
        return [self.chip(p) for p in range(self.chips)]

    def devices(self, spots):
        me = lax.axis_index("dp")
        at = self.pos(lax.div(me, 2), lax.div, jnp.where)
        core = me - 2 * lax.div(me, 2)
        found = []
        for dist, other in spots:
            chip = self.chip(lax.rem(at + dist % self.chips, self.chips), lax.div, jnp.where)
            found.append(2 * chip + (1 - core if other else core))
        return found, core


def ring_perm(ring, shift, cross):
    n = len(ring)
    pairs = []
    for at, chip in enumerate(ring):
        to = ring[(at + shift) % n]
        pairs += [(2 * chip + c, 2 * to + (c ^ cross)) for c in (0, 1)]
    return pairs


def _combine(terms):
    by = {}
    for k, v in terms:
        k %= ROT
        k = min(k, ROT - k)
        sign = 1
        if k > 9:
            k, sign = HALF - k, -1
        if k == 9:
            continue
        by.setdefault(k, []).append((sign, v))
    total = None
    for k, vs in sorted(by.items()):
        part, psign = None, 1
        for sign, v in vs:
            if part is None:
                part, psign = v, sign
            else:
                part = part + v if sign == psign else part - v
        if k:
            part = part * math.cos(k * math.pi / HALF)
        if total is None:
            total = part if psign > 0 else -part
        else:
            total = total + part if psign > 0 else total - part
    return total


def cos_transform(a):
    plus = [a[t] + a[HALF - t] for t in range(9)] + [a[9]]
    minus = [a[t] - a[HALF - t] for t in range(9)]
    out = [None] * 19
    for j in range(10):
        side = plus if j % 2 == 0 else minus
        even = _combine([(t * j, side[t]) for t in range(0, len(side), 2)])
        odd = _combine([(t * j, side[t]) for t in range(1, len(side), 2)])
        if odd is None:
            out[j] = out[HALF - j] = even
        else:
            out[j] = even + odd
            out[HALF - j] = even - odd
    return out


def sin_transform(b):
    plus = {t: b[t] + b[HALF - t] for t in range(1, 9)}
    plus[9] = b[9]
    minus = {t: b[t] - b[HALF - t] for t in range(1, 9)}
    out = [None] * 18
    for j in range(1, 10):
        side = plus if j % 2 else minus
        even = _combine([(9 - t * j, v) for t, v in side.items() if t % 2 == 0])
        odd = _combine([(9 - t * j, v) for t, v in side.items() if t % 2])
        if odd is None:
            odd = jnp.zeros_like(even)
        if even is None:
            even = jnp.zeros_like(odd)
        out[j] = odd + even
        if j != 9:
            out[HALF - j] = odd - even
    return out


def _residue(m):
    r = lax.rem(m, ROT)
    flip = r > HALF
    return jnp.where(flip, ROT - r, r), jnp.where(flip, -1.0, 1.0).astype(F32)


def _half_sign(shape):
    lane = lax.broadcasted_iota(jnp.int32, shape, len(shape) - 1)
    return jnp.where(lane < shape[-1] // 2, -1.0, 1.0).astype(F32)


def _forward(base, mp, piece, row, wo, ws, acc, energy):
    kh, q = piece.shape[1:]
    sign = _half_sign((kh, q))
    first = base * mp
    squares = jnp.zeros((kh, q), F32)
    for j in range(mp):
        m = first + j
        t, s = _residue(m)
        x = piece[row + j]
        wide = x.astype(F32)
        squares = squares + wide * wide
        swapped = (pltpu.roll(wide, q // 2, 1) * sign).astype(BF16)
        both = jnp.concatenate([x, swapped], axis=0)
        w = jnp.concatenate([wo[m], ws[m]], axis=0)
        y = lax.dot_general(both, w, (((1,), (1,)), ((), ())), preferred_element_type=F32)
        acc[t, :kh, :] += y[:kh]
        acc[t, kh:, :] += s * y[kh:]
    energy[...] += squares


def _forward_all(ring, spots, mp, wo, ws, pieces, acc, energy):
    at, _ = ring.devices(spots)
    for piece in pieces:
        for row in range(0, piece.shape[0], mp):
            if at:
                _forward(at.pop(0), mp, piece, row, wo, ws, acc, energy)


def _backward(m, table, wo, ws):
    t, s = _residue(m)
    w = jnp.concatenate([wo[m], ws[m]], axis=0)
    y = jnp.dot(table[t], w, preferred_element_type=F32)
    kh = y.shape[0] // 2
    turned = pltpu.roll(y[kh:], y.shape[1] // 2, 1) * (_half_sign((kh, y.shape[1])) * s)
    return y[:kh] + turned


def split_kernel(from_left, from_right, p_x, p_y, q_x, q_y):
    mp = p_x.shape[0]
    p_x[...], q_y[...] = from_left[:mp], from_left[mp:]
    q_x[...], p_y[...] = from_right[:mp], from_right[mp:]


def forward_kernel(ring, spots, mp, first, wo, ws, *refs):
    acc, energy = refs[-2:]
    if first:
        acc[...] = jnp.zeros_like(acc)
        energy[...] = jnp.zeros_like(energy)
    _forward_all(ring, spots, mp, wo, ws, refs, acc, energy)


def score_kernel(ring, spots, mp, wo, ws, *refs):
    w2, prior, _, _, acc, energy, real_out, imag_out, stats, scores = refs[2:]
    _forward_all(ring, spots, mp, wo, ws, refs, acc, energy)
    kh, n = scores.shape[1:]
    norm = lax.dot_general(
        energy[...], w2[...], (((1,), (1,)), ((), ())), precision=HIGHEST, preferred_element_type=F32
    )
    energy[...] = jnp.log(prior[...]) - 0.5 * norm
    tile = 8

    def scan_scores(i, top):
        at = pl.multiple_of(i * tile, tile)
        rows, rows_imag = pl.ds(at, tile), pl.ds(pl.multiple_of(kh + i * tile, tile), tile)
        p = cos_transform([acc[t, rows, :] for t in range(19)])
        q = sin_transform([None] + [acc[t, rows_imag, :] for t in range(1, HALF)])
        base = energy[rows, :]
        for j in range(19):
            pj = p[j] + base
            if j in (0, HALF):
                scores[j, rows, :] = pj
                top = jnp.maximum(top, pj)
            else:
                lo, hi = pj - q[j], pj + q[j]
                scores[j, rows, :] = lo
                scores[ROT - j, rows, :] = hi
                top = jnp.maximum(top, jnp.maximum(lo, hi))
        return top

    top = lax.fori_loop(0, kh // tile, scan_scores, jnp.full((tile, n), -jnp.inf, F32))
    top = jnp.max(top, axis=0, keepdims=True)

    def scan_exp(i, total):
        rows = pl.ds(pl.multiple_of(i * tile, tile), tile)
        u = [jnp.exp(scores[j, rows, :] - top) for j in range(ROT)]
        plus = [u[0]] + [u[j] + u[ROT - j] for j in range(1, HALF)] + [u[HALF]]
        minus = [None] + [u[j] - u[ROT - j] for j in range(1, HALF)]
        real = cos_transform(plus)
        imag = sin_transform(minus)
        for t in range(19):
            real_out[t, rows, :] = real[t]
        for t in range(1, HALF):
            imag_out[t - 1, rows, :] = imag[t]
        return total + real[0]

    total = lax.fori_loop(0, kh // tile, scan_exp, jnp.zeros((tile, n), F32))
    stats[0:1, :] = top
    stats[1:2, :] = jnp.sum(total, axis=0, keepdims=True)


def table_kernel(ring, spots, mp, wo, ws, real, imag, mine, other, w2, table, evidence, dpart, *outs):
    kh, n = real.shape[1:]
    theirs = pltpu.roll(jnp.broadcast_to(other[...].reshape(2, 1, n), (2, 8, n)).reshape(16, n), n // 2, 1)
    top_a, total_a = mine[0:1, :], mine[1:2, :]
    top_b, total_b = theirs[0:1, :], theirs[8:9, :]
    top = jnp.maximum(top_a, top_b)
    scale = jnp.exp(top_a - top)
    total = total_a * scale + total_b * jnp.exp(top_b - top)
    evidence[...] = top + jnp.log(total)
    scale = scale / total
    for t in range(19):
        table[t, :kh, :] = (real[t] * scale).astype(BF16)
        if 0 < t < HALF:
            table[t, kh:, :] = (imag[t - 1] * scale).astype(BF16)
        else:
            table[t, kh:, :] = jnp.zeros((kh, n), BF16)
    dpart[...] = jnp.dot(real[0] * scale, w2[...], precision=HIGHEST, preferred_element_type=F32)
    at, _ = ring.devices(spots)
    for base, out in zip(at, outs):
        for j in range(mp):
            out[j] = _backward(base * mp + j, table, wo, ws).astype(out.dtype)
    for out in outs[:2]:
        out[mp] = _split(dpart[...])


def numer_kernel(ring, spots, mp, wo, ws, table, *outs):
    at, _ = ring.devices(spots)
    for base, out in zip(at, outs):
        for j in range(mp):
            out[j] = _backward(base * mp + j, table, wo, ws)


def _split(x):
    lead = x.astype(BF16)
    rest = (x - lead.astype(F32)).astype(BF16)
    lane = lax.broadcasted_iota(jnp.int32, x.shape, 1)
    return jnp.where(lane < x.shape[1] // 2, lead.astype(F32), rest.astype(F32)).astype(BF16)


def _join(row):
    wide = row.astype(F32)
    return wide + pltpu.roll(wide, row.shape[1] // 2, 1)


def add_kernel(part_x, part_y, got_x, got_y, *refs):
    n = part_x.shape[0]
    tails = got_x.shape[0] > n
    out_x, out_y = refs[1:3] if tails else refs
    for part, got, out in ((part_x, got_x, out_x), (part_y, got_y, out_y)):
        out[:n] = (part[...] + got[:n].astype(F32)).astype(BF16)
        if tails:
            out[n] = got[n]
    if tails:
        refs[3][...] = refs[0][...] + (_join(got_x[n]) + _join(got_y[n]))


def own_kernel(part_x, part_y, p_x, p_y, q_x, q_y, dsum, own, far):
    mp = own.shape[0]
    inv = 1.0 / (1.0 + dsum[...] + _join(p_x[mp]))
    for j in range(mp):
        own[j] = (part_x[j] + p_x[j].astype(F32) + q_x[j].astype(F32)) * inv
        far[j] = ((part_y[j] + p_y[j].astype(F32) + q_y[j].astype(F32)) * inv).astype(BF16)


def final_kernel(ring, own, own_x, out):
    kh = own.shape[1]
    _, c = ring.devices([])
    out[:, pl.ds(pl.multiple_of(c * kh, kh), kh), :] = own[...]
    out[:, pl.ds(pl.multiple_of((1 - c) * kh, kh), kh), :] = own_x[...].astype(F32)


def _call(kernel, operands, outs, scratch=(), aliases=None, keep=True):
    return pl.pallas_call(
        kernel,
        out_shape=[pltpu.VMEM(o.shape, o.dtype) for o in outs] if keep else outs,
        in_specs=[pl.BlockSpec(memory_space=pltpu.VMEM)] * len(operands),
        out_specs=[pl.BlockSpec(memory_space=pltpu.VMEM)] * len(outs),
        scratch_shapes=scratch,
        input_output_aliases=aliases or {},
        compiler_params=pltpu.CompilerParams(vmem_limit_bytes=VMEM_LIMIT),
        cost_estimate=pl.CostEstimate(flops=1, bytes_accessed=1, transcendentals=0),
    )(*[pltpu.with_memory_space_constraint(a, pltpu.VMEM) for a in operands])


def ctf_table(defocus, radial):
    radius = (jnp.arange(radial, dtype=F32) + 1.0) / radial
    phase = 20.0 * defocus[:, None] * radius[None, :] ** 2
    return -(0.995 * jnp.sin(phase) + 0.1 * jnp.cos(phase))


def shards(ring, particles, refs, ctf_group, defocus, class_prior, cycle_weight):
    chips = ring.chips
    order = ring.order()
    opposite = chips // 2
    nl, _, q = particles.shape
    mp, k, _ = refs.shape
    kh = k // 2
    n2 = 2 * nl
    c = lax.rem(lax.axis_index("dp"), 2)

    send = lambda a, shift, cross: lax.ppermute(a, "dp", ring_perm(order, shift, cross))
    core_swap = lambda a: lax.ppermute(a, "dp", [(i, i ^ 1) for i in range(2 * chips)])
    tie = lax.optimization_barrier

    near = lax.dynamic_slice_in_dim(refs, c * kh, kh, axis=1)
    far = lax.dynamic_slice_in_dim(refs, (1 - c) * kh, kh, axis=1)
    group_x = core_swap(ctf_group)
    chunk = jnp.concatenate([near, core_swap(far)], axis=0)
    chunk, particles, defocus, cycle_weight, ctf_group = tie((chunk, particles, defocus, cycle_weight, ctf_group))
    from_left, from_right = send(chunk, 1, 0), send(chunk, -1, 0)
    particles_x = with_layout_constraint(core_swap(particles), Layout(major_to_minor=(0, 1, 2)))

    ctf = ctf_table(defocus, q // 2)
    gains = cycle_weight[None, :] * ctf
    gain_table = jnp.concatenate([gains, gains], axis=1)
    square_table = jnp.concatenate([gains * ctf, gains * ctf], axis=1)
    index = jnp.arange(defocus.shape[0], dtype=jnp.int32)[None, :]
    groups = jnp.concatenate([ctf_group, group_x])
    onehot = (groups[:, None] == index).astype(F32)
    both = jnp.dot(onehot, jnp.concatenate([gain_table, square_table], axis=1), precision=HIGHEST)
    gain, w2 = both[:, :q], both[:, q:]
    weigh = lambda a, g: jnp.transpose((a.astype(F32) * g[:, None, :]).astype(BF16), (1, 0, 2))
    wo = weigh(particles, gain[:nl])
    prior = lax.dynamic_slice_in_dim(class_prior, c * kh, kh, axis=0)[:, None]
    prior = jnp.broadcast_to(prior, (kh, n2))

    shape = jax.ShapeDtypeStruct
    acc_shapes = [shape((19, 2 * kh, n2), F32), shape((kh, q), F32)]
    from_left, from_right, wo, particles_x = tie((from_left, from_right, wo, particles_x))
    p_x, p_y, q_x, q_y = _call(split_kernel, [from_left, from_right], [shape((mp, kh, q), BF16)] * 4)
    pieces, where = [chunk], [(0, 0), (0, 1)]
    acc = ws = None
    for step in range(1, opposite):
        pieces = pieces + [p_x, p_y, q_x, q_y]
        where = where + [(-step, 0), (step, 1), (step, 0), (-step, 1)]
        if ws is None:
            ws = weigh(particles_x, gain[nl:])
        elif acc is None:
            p_x, p_y, ws = tie((p_x, p_y, ws))
        else:
            p_x, p_y, acc = tie((p_x, p_y, acc))
        p_x, p_y = send(p_x, 1, 0), send(p_y, -1, 0)
        if step < opposite - 1:
            q_x, q_y = send(q_x, -1, 0), send(q_y, 1, 0)
        if step == 1 and opposite > 2:
            continue
        count = len(pieces)
        acc = _call(
            functools.partial(forward_kernel, ring, where, mp, acc is None),
            [wo, ws] + pieces + list(acc or []),
            acc_shapes,
            aliases={2 + count: 0, 3 + count: 1} if acc else None,
        )
        pieces, where = [], []

    where = [(opposite, 0), (opposite, 1)]
    _, _, real, imag, stats = _call(
        functools.partial(score_kernel, ring, where, mp),
        [wo, ws, p_x, p_y, w2, prior] + list(acc),
        acc_shapes + [shape((19, kh, n2), F32), shape((17, kh, n2), F32), shape((2, n2), F32)],
        aliases={6: 0, 7: 1},
        scratch=[pltpu.VMEM((ROT, kh, n2), F32)],
    )
    stats_x = core_swap(stats)

    piece = shape((mp, kh, q), BF16)
    piece_d = shape((mp + 1, kh, q), BF16)
    wide = shape((mp, kh, q), F32)
    dsum_shape = shape((kh, q), F32)
    far = opposite - 1
    table, evidence, dsum, p_x, p_y, q_x, q_y = _call(
        functools.partial(table_kernel, ring, [(opposite, 0), (opposite, 1), (-far, 0), (far, 1)], mp),
        [wo, ws, real, imag, stats, stats_x, w2],
        [shape((19, 2 * kh, n2), BF16), shape((1, n2), F32), dsum_shape, piece_d, piece_d, piece, piece],
    )
    for dist in range(far, -1, -1):
        p_x, p_y = send(p_x, 1, 0), send(p_y, -1, 0)
        if dist:
            q_x, q_y = send(q_x, -1, 0), send(q_y, 1, 0)
            spots = [(dist, 0), (-dist, 1), (-(dist - 1), 0), (dist - 1, 1)]
            px, py, qx, qy = _call(functools.partial(numer_kernel, ring, spots, mp), [wo, ws, table], [wide] * 4)
            p_x, p_y, dsum = _call(add_kernel, [px, py, p_x, p_y, dsum], [piece_d, piece_d, dsum_shape])
            if dist > 1:
                q_x, q_y = _call(add_kernel, [qx, qy, q_x, q_y], [piece, piece])
    own, far = _call(own_kernel, [qx, qy, p_x, p_y, q_x, q_y, dsum], [shape((mp, kh, q), F32), piece])
    new_refs = _call(
        functools.partial(final_kernel, ring), [own, core_swap(far)], [shape((mp, k, q), F32)], keep=False
    )[0]
    return new_refs, evidence[0, :nl]


def solution(mesh):
    in_specs = (
        P(("groups", "dp"), None, None),
        P("dp", "groups", None),
        P(("groups", "dp")),
        P("groups"),
        P("groups"),
        P(),
    )
    out_specs = (P("dp", "groups", None), P(("groups", "dp")))
    body = functools.partial(shards, Ring(mesh))
    return jax.shard_map(body, mesh=mesh, in_specs=in_specs, out_specs=out_specs, check_vma=False)
```

```python
import functools
import math

import jax
import jax.numpy as jnp
from jax import lax
from jax.experimental import pallas as pl
from jax.experimental.layout import Layout, with_layout_constraint
from jax.experimental.pallas import tpu as pltpu
from jax.sharding import PartitionSpec as P

ROT = 36
HALF = ROT // 2
HIGHEST = lax.Precision.HIGHEST
F32 = jnp.float32
BF16 = jnp.bfloat16
VMEM_LIMIT = 40 * 1024 * 1024


class Ring:
    def __init__(self, mesh):
        self.chips = mesh.shape["dp"] // 2
        wide = 2
        coords = [getattr(d, "coords", None) for d in mesh.devices.reshape(-1, 2 * self.chips)[0]]
        if all(c is not None for c in coords):
            wide = len({c[0] for c in coords})
        self.wide = wide if self.chips % wide == 0 else 1
        self.deep = self.chips // self.wide

    def chip(self, pos, div=lambda a, b: a // b, pick=lambda c, a, b: a if c else b):
        if self.wide == 1:
            return pos
        row = self.wide - 1
        z = div(pos, row)
        i = pos - z * row
        x = pick(z - 2 * div(z, 2) == 0, 1 + i, row - i)
        back = self.deep - 1 - (pos - self.deep * row)
        return pick(pos < self.deep * row, z * self.wide + x, back * self.wide)

    def pos(self, chip, div=lambda a, b: a // b, pick=lambda c, a, b: a if c else b):
        if self.wide == 1:
            return chip
        row = self.wide - 1
        z = div(chip, self.wide)
        x = chip - z * self.wide
        i = pick(z - 2 * div(z, 2) == 0, x - 1, row - x)
        return pick(x == 0, self.deep * row + self.deep - 1 - z, z * row + i)

    def order(self):
        return [self.chip(p) for p in range(self.chips)]

    def devices(self, spots):
        me = lax.axis_index("dp")
        at = self.pos(lax.div(me, 2), lax.div, jnp.where)
        core = me - 2 * lax.div(me, 2)
        found = []
        for dist, other in spots:
            chip = self.chip(lax.rem(at + dist % self.chips, self.chips), lax.div, jnp.where)
            found.append(2 * chip + (1 - core if other else core))
        return found, core


def ring_perm(ring, shift, cross):
    n = len(ring)
    pairs = []
    for at, chip in enumerate(ring):
        to = ring[(at + shift) % n]
        pairs += [(2 * chip + c, 2 * to + (c ^ cross)) for c in (0, 1)]
    return pairs


def _combine(terms):
    by = {}
    for k, v in terms:
        k %= ROT
        k = min(k, ROT - k)
        sign = 1
        if k > 9:
            k, sign = HALF - k, -1
        if k == 9:
            continue
        by.setdefault(k, []).append((sign, v))
    total = None
    for k, vs in sorted(by.items()):
        part, psign = None, 1
        for sign, v in vs:
            if part is None:
                part, psign = v, sign
            else:
                part = part + v if sign == psign else part - v
        if k:
            part = part * math.cos(k * math.pi / HALF)
        if total is None:
            total = part if psign > 0 else -part
        else:
            total = total + part if psign > 0 else total - part
    return total


def cos_transform(a):
    plus = [a[t] + a[HALF - t] for t in range(9)] + [a[9]]
    minus = [a[t] - a[HALF - t] for t in range(9)]
    out = [None] * 19
    for j in range(10):
        side = plus if j % 2 == 0 else minus
        even = _combine([(t * j, side[t]) for t in range(0, len(side), 2)])
        odd = _combine([(t * j, side[t]) for t in range(1, len(side), 2)])
        if odd is None:
            out[j] = out[HALF - j] = even
        else:
            out[j] = even + odd
            out[HALF - j] = even - odd
    return out


def sin_transform(b):
    plus = {t: b[t] + b[HALF - t] for t in range(1, 9)}
    plus[9] = b[9]
    minus = {t: b[t] - b[HALF - t] for t in range(1, 9)}
    out = [None] * 18
    for j in range(1, 10):
        side = plus if j % 2 else minus
        even = _combine([(9 - t * j, v) for t, v in side.items() if t % 2 == 0])
        odd = _combine([(9 - t * j, v) for t, v in side.items() if t % 2])
        if odd is None:
            odd = jnp.zeros_like(even)
        if even is None:
            even = jnp.zeros_like(odd)
        out[j] = odd + even
        if j != 9:
            out[HALF - j] = odd - even
    return out


def _residue(m):
    r = lax.rem(m, ROT)
    flip = r > HALF
    return jnp.where(flip, ROT - r, r), jnp.where(flip, -1.0, 1.0).astype(F32)


def _half_sign(shape):
    lane = lax.broadcasted_iota(jnp.int32, shape, len(shape) - 1)
    return jnp.where(lane < shape[-1] // 2, -1.0, 1.0).astype(F32)


def _forward(base, mp, piece, row, wo, ws, acc, energy):
    kh, q = piece.shape[1:]
    sign = _half_sign((kh, q))
    first = base * mp
    squares = jnp.zeros((kh, q), F32)
    for j in range(mp):
        m = first + j
        t, s = _residue(m)
        x = piece[row + j]
        wide = x.astype(F32)
        squares = squares + wide * wide
        swapped = (pltpu.roll(wide, q // 2, 1) * sign).astype(BF16)
        both = jnp.concatenate([x, swapped], axis=0)
        w = jnp.concatenate([wo[m], ws[m]], axis=0)
        y = lax.dot_general(both, w, (((1,), (1,)), ((), ())), preferred_element_type=F32)
        acc[t, :kh, :] += y[:kh]
        acc[t, kh:, :] += s * y[kh:]
    energy[...] += squares


def _forward_all(ring, spots, mp, wo, ws, pieces, acc, energy):
    at, _ = ring.devices(spots)
    for piece in pieces:
        for row in range(0, piece.shape[0], mp):
            if at:
                _forward(at.pop(0), mp, piece, row, wo, ws, acc, energy)


def _backward(m, table, wo, ws):
    t, s = _residue(m)
    w = jnp.concatenate([wo[m], ws[m]], axis=0)
    y = jnp.dot(table[t], w, preferred_element_type=F32)
    kh = y.shape[0] // 2
    turned = pltpu.roll(y[kh:], y.shape[1] // 2, 1) * (_half_sign((kh, y.shape[1])) * s)
    return y[:kh] + turned


def split_kernel(from_left, from_right, p_x, p_y, q_x, q_y):
    mp = p_x.shape[0]
    p_x[...], q_y[...] = from_left[:mp], from_left[mp:]
    q_x[...], p_y[...] = from_right[:mp], from_right[mp:]


def forward_kernel(ring, spots, mp, first, wo, ws, *refs):
    acc, energy = refs[-2:]
    if first:
        acc[...] = jnp.zeros_like(acc)
        energy[...] = jnp.zeros_like(energy)
    _forward_all(ring, spots, mp, wo, ws, refs, acc, energy)


def score_kernel(ring, spots, mp, wo, ws, *refs):
    w2, prior, _, _, acc, energy, real_out, imag_out, stats, scores = refs[2:]
    _forward_all(ring, spots, mp, wo, ws, refs, acc, energy)
    kh, n = scores.shape[1:]
    norm = lax.dot_general(
        energy[...], w2[...], (((1,), (1,)), ((), ())), precision=HIGHEST, preferred_element_type=F32
    )
    energy[...] = jnp.log(prior[...]) - 0.5 * norm
    tile = 8

    def scan_scores(i, top):
        at = pl.multiple_of(i * tile, tile)
        rows, rows_imag = pl.ds(at, tile), pl.ds(pl.multiple_of(kh + i * tile, tile), tile)
        p = cos_transform([acc[t, rows, :] for t in range(19)])
        q = sin_transform([None] + [acc[t, rows_imag, :] for t in range(1, HALF)])
        base = energy[rows, :]
        for j in range(19):
            pj = p[j] + base
            if j in (0, HALF):
                scores[j, rows, :] = pj
                top = jnp.maximum(top, pj)
            else:
                lo, hi = pj - q[j], pj + q[j]
                scores[j, rows, :] = lo
                scores[ROT - j, rows, :] = hi
                top = jnp.maximum(top, jnp.maximum(lo, hi))
        return top

    top = lax.fori_loop(0, kh // tile, scan_scores, jnp.full((tile, n), -jnp.inf, F32))
    top = jnp.max(top, axis=0, keepdims=True)

    def scan_exp(i, total):
        rows = pl.ds(pl.multiple_of(i * tile, tile), tile)
        u = [jnp.exp(scores[j, rows, :] - top) for j in range(ROT)]
        plus = [u[0]] + [u[j] + u[ROT - j] for j in range(1, HALF)] + [u[HALF]]
        minus = [None] + [u[j] - u[ROT - j] for j in range(1, HALF)]
        real = cos_transform(plus)
        imag = sin_transform(minus)
        for t in range(19):
            real_out[t, rows, :] = real[t]
        for t in range(1, HALF):
            imag_out[t - 1, rows, :] = imag[t]
        return total + real[0]

    total = lax.fori_loop(0, kh // tile, scan_exp, jnp.zeros((tile, n), F32))
    stats[0:1, :] = top
    stats[1:2, :] = jnp.sum(total, axis=0, keepdims=True)


def table_kernel(ring, spots, mp, wo, ws, real, imag, mine, other, w2, table, evidence, dpart, *outs):
    kh, n = real.shape[1:]
    theirs = pltpu.roll(jnp.broadcast_to(other[...].reshape(2, 1, n), (2, 8, n)).reshape(16, n), n // 2, 1)
    top_a, total_a = mine[0:1, :], mine[1:2, :]
    top_b, total_b = theirs[0:1, :], theirs[8:9, :]
    top = jnp.maximum(top_a, top_b)
    scale = jnp.exp(top_a - top)
    total = total_a * scale + total_b * jnp.exp(top_b - top)
    evidence[...] = top + jnp.log(total)
    scale = scale / total
    for t in range(19):
        table[t, :kh, :] = (real[t] * scale).astype(BF16)
        if 0 < t < HALF:
            table[t, kh:, :] = (imag[t - 1] * scale).astype(BF16)
        else:
            table[t, kh:, :] = jnp.zeros((kh, n), BF16)
    dpart[...] = jnp.dot(real[0] * scale, w2[...], precision=HIGHEST, preferred_element_type=F32)
    at, _ = ring.devices(spots)
    for base, out in zip(at, outs):
        for j in range(mp):
            out[j] = _backward(base * mp + j, table, wo, ws).astype(out.dtype)
    for out in outs[:2]:
        out[mp] = _split(dpart[...])
    for out in outs[2:]:
        out[mp:] = jnp.zeros_like(out[mp:])


def numer_kernel(ring, spots, mp, wo, ws, table, *outs):
    at, _ = ring.devices(spots)
    for base, out in zip(at, outs):
        for j in range(mp):
            out[j] = _backward(base * mp + j, table, wo, ws)


def _split(x):
    lead = x.astype(BF16)
    rest = (x - lead.astype(F32)).astype(BF16)
    lane = lax.broadcasted_iota(jnp.int32, x.shape, 1)
    return jnp.where(lane < x.shape[1] // 2, lead.astype(F32), rest.astype(F32)).astype(BF16)


def _join(row):
    wide = row.astype(F32)
    return wide + pltpu.roll(wide, row.shape[1] // 2, 1)


def add_kernel(part_x, part_y, got_x, got_y, *refs):
    n = part_x.shape[0]
    tails = len(refs) == 4
    out_x, out_y = refs[1:3] if tails else refs
    for part, got, out in ((part_x, got_x, out_x), (part_y, got_y, out_y)):
        out[:n] = (part[...] + got[:n].astype(F32)).astype(BF16)
        out[n:] = got[n:]
    if tails:
        refs[3][...] = refs[0][...] + (_join(got_x[n]) + _join(got_y[n]))


def own_kernel(part_x, part_y, p_x, p_y, q_x, q_y, dsum, own, far):
    mp = own.shape[0]
    inv = 1.0 / (1.0 + dsum[...] + _join(p_x[mp]))
    for j in range(mp):
        own[j] = (part_x[j] + p_x[j].astype(F32) + q_x[j].astype(F32)) * inv
        far[j] = ((part_y[j] + p_y[j].astype(F32) + q_y[j].astype(F32)) * inv).astype(BF16)


def final_kernel(ring, own, own_x, out):
    kh = own.shape[1]
    _, c = ring.devices([])
    out[:, pl.ds(pl.multiple_of(c * kh, kh), kh), :] = own[...]
    out[:, pl.ds(pl.multiple_of((1 - c) * kh, kh), kh), :] = own_x[...].astype(F32)


def _call(kernel, operands, outs, scratch=(), aliases=None, keep=True):
    return pl.pallas_call(
        kernel,
        out_shape=[pltpu.VMEM(o.shape, o.dtype) for o in outs] if keep else outs,
        in_specs=[pl.BlockSpec(memory_space=pltpu.VMEM)] * len(operands),
        out_specs=[pl.BlockSpec(memory_space=pltpu.VMEM)] * len(outs),
        scratch_shapes=scratch,
        input_output_aliases=aliases or {},
        compiler_params=pltpu.CompilerParams(vmem_limit_bytes=VMEM_LIMIT),
        cost_estimate=pl.CostEstimate(flops=1, bytes_accessed=1, transcendentals=0),
    )(*[pltpu.with_memory_space_constraint(a, pltpu.VMEM) for a in operands])


def ctf_table(defocus, radial):
    radius = (jnp.arange(radial, dtype=F32) + 1.0) / radial
    phase = 20.0 * defocus[:, None] * radius[None, :] ** 2
    return -(0.995 * jnp.sin(phase) + 0.1 * jnp.cos(phase))


def shards(ring, particles, refs, ctf_group, defocus, class_prior, cycle_weight):
    chips = ring.chips
    order = ring.order()
    opposite = chips // 2
    nl, _, q = particles.shape
    mp, k, _ = refs.shape
    kh = k // 2
    n2 = 2 * nl
    c = lax.rem(lax.axis_index("dp"), 2)

    send = lambda a, shift, cross: lax.ppermute(a, "dp", ring_perm(order, shift, cross))
    core_swap = lambda a: lax.ppermute(a, "dp", [(i, i ^ 1) for i in range(2 * chips)])
    tie = lax.optimization_barrier

    near = lax.dynamic_slice_in_dim(refs, c * kh, kh, axis=1)
    far = lax.dynamic_slice_in_dim(refs, (1 - c) * kh, kh, axis=1)
    group_x = core_swap(ctf_group)
    chunk = jnp.concatenate([near, core_swap(far)], axis=0)
    chunk, particles, defocus, cycle_weight, ctf_group = tie((chunk, particles, defocus, cycle_weight, ctf_group))
    from_left, from_right = send(chunk, 1, 0), send(chunk, -1, 0)
    particles_x = with_layout_constraint(core_swap(particles), Layout(major_to_minor=(0, 1, 2)))

    ctf = ctf_table(defocus, q // 2)
    gains = cycle_weight[None, :] * ctf
    gain_table = jnp.concatenate([gains, gains], axis=1)
    square_table = jnp.concatenate([gains * ctf, gains * ctf], axis=1)
    index = jnp.arange(defocus.shape[0], dtype=jnp.int32)[None, :]
    groups = jnp.concatenate([ctf_group, group_x])
    onehot = (groups[:, None] == index).astype(F32)
    both = jnp.dot(onehot, jnp.concatenate([gain_table, square_table], axis=1), precision=HIGHEST)
    gain, w2 = both[:, :q], both[:, q:]
    weigh = lambda a, g: jnp.transpose((a.astype(F32) * g[:, None, :]).astype(BF16), (1, 0, 2))
    wo = weigh(particles, gain[:nl])
    prior = lax.dynamic_slice_in_dim(class_prior, c * kh, kh, axis=0)[:, None]
    prior = jnp.broadcast_to(prior, (kh, n2))

    shape = jax.ShapeDtypeStruct
    acc_shapes = [shape((19, 2 * kh, n2), F32), shape((kh, q), F32)]
    from_left, from_right, wo, particles_x = tie((from_left, from_right, wo, particles_x))
    p_x, p_y, q_x, q_y = _call(split_kernel, [from_left, from_right], [shape((mp, kh, q), BF16)] * 4)
    pieces, where = [chunk], [(0, 0), (0, 1)]
    acc = ws = None
    for step in range(1, opposite):
        pieces = pieces + [p_x, p_y, q_x, q_y]
        where = where + [(-step, 0), (step, 1), (step, 0), (-step, 1)]
        if ws is None:
            ws = weigh(particles_x, gain[nl:])
        elif acc is None:
            p_x, p_y, ws = tie((p_x, p_y, ws))
        else:
            p_x, p_y, acc = tie((p_x, p_y, acc))
        p_x, p_y = send(p_x, 1, 0), send(p_y, -1, 0)
        if step < opposite - 1:
            q_x, q_y = send(q_x, -1, 0), send(q_y, 1, 0)
        if step == 1 and opposite > 2:
            continue
        count = len(pieces)
        acc = _call(
            functools.partial(forward_kernel, ring, where, mp, acc is None),
            [wo, ws] + pieces + list(acc or []),
            acc_shapes,
            aliases={2 + count: 0, 3 + count: 1} if acc else None,
        )
        pieces, where = [], []

    where = [(opposite, 0), (opposite, 1)]
    _, _, real, imag, stats = _call(
        functools.partial(score_kernel, ring, where, mp),
        [wo, ws, p_x, p_y, w2, prior] + list(acc),
        acc_shapes + [shape((19, kh, n2), F32), shape((17, kh, n2), F32), shape((2, n2), F32)],
        aliases={6: 0, 7: 1},
        scratch=[pltpu.VMEM((ROT, kh, n2), F32)],
    )
    stats_x = core_swap(stats)

    piece = shape((mp, kh, q), BF16)
    piece_d = shape((mp + 1, kh, q), BF16)
    wide = shape((mp, kh, q), F32)
    piece_q = shape((mp + 1, kh, q), BF16)
    dsum_shape = shape((kh, q), F32)
    far = opposite - 1
    table, evidence, dsum, p_x, p_y, q_x, q_y = _call(
        functools.partial(table_kernel, ring, [(opposite, 0), (opposite, 1), (-far, 0), (far, 1)], mp),
        [wo, ws, real, imag, stats, stats_x, w2],
        [shape((19, 2 * kh, n2), BF16), shape((1, n2), F32), dsum_shape, piece_d, piece_d, piece_q, piece_q],
    )
    for dist in range(far, -1, -1):
        p_x, p_y = send(p_x, 1, 0), send(p_y, -1, 0)
        if dist:
            q_x, q_y = send(q_x, -1, 0), send(q_y, 1, 0)
            spots = [(dist, 0), (-dist, 1), (-(dist - 1), 0), (dist - 1, 1)]
            px, py, qx, qy = _call(functools.partial(numer_kernel, ring, spots, mp), [wo, ws, table], [wide] * 4)
            p_x, p_y, dsum = _call(add_kernel, [px, py, p_x, p_y, dsum], [piece_d, piece_d, dsum_shape])
            if dist > 1:
                q_x, q_y = _call(add_kernel, [qx, qy, q_x, q_y], [piece_q, piece_q])
    own, far = _call(own_kernel, [qx, qy, p_x, p_y, q_x, q_y, dsum], [shape((mp, kh, q), F32), piece])
    new_refs = _call(
        functools.partial(final_kernel, ring), [own, core_swap(far)], [shape((mp, k, q), F32)], keep=False
    )[0]
    return new_refs, evidence[0, :nl]


def solution(mesh):
    in_specs = (
        P(("groups", "dp"), None, None),
        P("dp", "groups", None),
        P(("groups", "dp")),
        P("groups"),
        P("groups"),
        P(),
    )
    out_specs = (P("dp", "groups", None), P(("groups", "dp")))
    body = functools.partial(shards, Ring(mesh))
    return jax.shard_map(body, mesh=mesh, in_specs=in_specs, out_specs=out_specs, check_vma=False)
```
